32 devices in a mesh: rep: 2 (over y), ctx: 16 (over z, x, core).
Axes of the slice: x: 2, y: 2, z: 4, core: 2. Of those that a mesh axis runs over, the one named last changes fastest.
Arguments:
- resid: bfloat16 [512, 8192], P('rep', 'ctx'), parts along dimension 0, may hold values from -6 to 6
- prefix_values: bfloat16 [4096, 8192], P(('rep', 'ctx')), parts along dimension 0, may hold values from -6 to 6
- tail_values: bfloat16 [32, 48, 8192], P('rep', None, 'ctx'), parts along dimension 0, may hold values from -6 to 6
- tail_lengths: int32 [32], P('rep'), parts along dimension 0, may hold values from 0 to 48, as said below
- norm_gain: float32 [8192], replicated, may hold values from 0.1 to 1.9
- in_weight: bfloat16 [3, 8192, 8192], P(None, None, 'ctx'), may hold values from -0.0625 to 0.0625
- skip_gain: float32 [8192], replicated, may hold values from -1 to 1
- mode_residues: float32 [8, 8192], replicated, may hold values from -4 to 4
- mode_rates: float32 [8, 8192], replicated, may hold values from 0.000118371216 to 0.1
- out_weight: bfloat16 [8192, 8192], P(None, 'ctx'), may hold values from -0.0625 to 0.0625
- mlp_gain: float32 [8192], replicated, may hold values from 0.1 to 1.9
- gate_weight: bfloat16 [8192, 16384], P(None, 'ctx'), may hold values from -0.0625 to 0.0625
- up_weight: bfloat16 [8192, 16384], P(None, 'ctx'), may hold values from -0.0625 to 0.0625
- down_weight: bfloat16 [16384, 8192], P('ctx'), may hold values from -0.046875 to 0.046875
Outputs:
- output: bfloat16 [512, 8192], P(('rep', 'ctx')), parts along dimension 0
The draws below stay inside these ranges and needn't reach their ends.
There are 2 independent parts, one for each index of `rep`. The reference program is written for one: setup_inputs(seed, part) draws one part's arguments, and reference() takes and returns one part's arrays. A program takes and returns all parts, laid end to end along the dimension named above; an argument that names none is the same for every part. Nothing has to cross between parts.
Inputs may be any that keep to these rules, and one draw needn't show every extreme that they name: `tail_lengths`: at least one continuation has all 48 tail slots live.
All inputs are finite; a program needn't handle non-finite values.
Results may differ from the reference program's by a relative error of at most 0.012.
Values may be sent and summed in bfloat16 or wider, within the bound.
A program may use at most 192 MiB of HBM per device.

```python
import math
import jax
import jax.numpy as jnp
from jax import lax

D = 8192
FF = 16384
MODES = 8
W = 16
BRANCHES = 16
TAIL = 48
PROMPT_DEV = 128
PROMPT = 2048
ROWS = 256
N_CTX = 16


def draw_tail_lengths(key, part):
    first_key, second_key = jax.random.split(jax.random.fold_in(key, 11))
    lengths = jax.random.randint(first_key, (BRANCHES,), 0, TAIL + 1)
    chosen = jax.random.randint(second_key, (), 0, BRANCHES)
    return jnp.where(jnp.arange(BRANCHES) == chosen, TAIL, lengths).astype(jnp.int32)


def block_scale(stream_key, extent, cuts, least, high):
    level = 1.0
    for dim, blocks in cuts:
        heights = jax.random.uniform(jax.random.fold_in(jax.random.fold_in(stream_key, 6), dim), (blocks,), jnp.float32, least / len(cuts), high / len(cuts))
        level = level * jnp.repeat(jnp.exp(heights), extent[dim] // blocks).reshape((-1,) + (1,) * (len(extent) - 1 - dim))
    return level


def centred(rng, dims, scale, reach, cuts=(), held_as=jnp.bfloat16):
    values = jax.random.normal(rng, dims, jnp.float32) * scale
    if len(cuts) > 0:
        values = block_scale(rng, dims, cuts, -0.22, 0.18) * values
    return jnp.clip(values, min=-reach, max=reach).astype(held_as)


def setup_inputs(seed: int = 0, part: int = 0) -> dict:
    key_list = jax.random.split(jax.random.key(seed), 15)
    part_splits = jax.random.split(jax.random.fold_in(key_list[14], part), 15)
    return {
        "resid": centred(part_splits[0], (ROWS, D), 1.0, 6.0, ((1, 16),)),
        "prefix_values": centred(part_splits[1], (PROMPT, D), 1.0, 6.0, ((0, 16),)),
        "tail_values": centred(part_splits[2], (BRANCHES, TAIL, D), 1.0, 6.0, ((2, 16),)),
        "tail_lengths": draw_tail_lengths(jax.random.fold_in(jax.random.fold_in(key_list[14], part), 71), part),
        "norm_gain": jnp.clip(1.0 + 0.18 * jax.random.normal(key_list[4], (D,), jnp.float32), 0.1, 1.9),
        "in_weight": centred(key_list[5], (3, D, D), D ** -0.5, 0.0625, ((2, 16),)),
        "skip_gain": jnp.clip(jax.random.uniform(key_list[6], (D,), jnp.float32, -1.0, 1.0), -1.0, 1.0),
        "mode_residues": centred(key_list[7], (MODES, D), 1.0, 4.0, (), jnp.float32),
        "mode_rates": jnp.clip(jnp.exp(jax.random.uniform(key_list[8], (MODES, D), jnp.float32, math.log(0.000118371216), math.log(0.1))), 0.000118371216, 0.1),
        "out_weight": centred(key_list[9], (D, D), D ** -0.5, 0.0625, ((1, 16),)),
        "mlp_gain": jnp.clip(1.0 + 0.18 * jax.random.normal(key_list[10], (D,), jnp.float32), 0.1, 1.9),
        "gate_weight": centred(key_list[11], (D, FF), D ** -0.5, 0.0625, ((1, 16),)),
        "up_weight": centred(key_list[12], (D, FF), D ** -0.5, 0.0625, ((1, 16),)),
        "down_weight": centred(key_list[13], (FF, D), FF ** -0.5, 0.046875, ((0, 16),)),
    }


def rms_scale(values, gain):
    values = values.astype(jnp.float32)
    inverse = lax.rsqrt(lax.optimization_barrier(jnp.mean(values * values, axis=-1, keepdims=True)) + 1e-05)
    return (values * inverse * gain).astype(jnp.bfloat16)

def filter_taps(residues, rates, length):
    lags = jnp.arange(length).astype(jnp.float32)
    weights = residues * jnp.sqrt(rates)
    result = jnp.zeros((length, residues.shape[1]), jnp.float32)
    for mode in range(residues.shape[0]):
        result = result + weights[mode][None, :] * jnp.exp(-rates[mode][None, :] * lags[:, None])
    return result

def lag_toeplitz(near_taps, tail_slots, window):
    positions = tail_slots + window
    row_pos = jnp.arange(window)[:, None, None]
    col_pos = jnp.arange(positions)[None, :, None]
    lag_pos = jnp.arange(positions)[None, None, :]
    picked = (lag_pos == tail_slots + row_pos - col_pos) & (col_pos <= tail_slots + row_pos)
    return jnp.einsum('jpn,nc->jpc', picked.astype(jnp.float32), near_taps.astype(jnp.float32))

def mode_states(values, distance, rates):
    values = values.astype(jnp.float32)
    stacked = []
    for mode in range(rates.shape[0]):
        stacked.append(lax.optimization_barrier(jnp.sum(jnp.exp(-rates[mode][None, :] * distance[:, None]) * values, axis=0)))
    return jnp.stack(stacked)

def expand_states(states, residues, rates, window):
    lags = jnp.arange(window).astype(jnp.float32)
    weights = residues * jnp.sqrt(rates) * states
    result = jnp.zeros((window, states.shape[1]), jnp.float32)
    for mode in range(states.shape[0]):
        result = result + weights[mode][None, :] * jnp.exp(-rates[mode][None, :] * lags[:, None])
    return result

def reference(resid, prefix_values, tail_values, tail_lengths, norm_gain, in_weight, skip_gain, mode_residues, mode_rates, out_weight, mlp_gain, gate_weight, up_weight, down_weight):
    normed = rms_scale(resid, norm_gain)
    first_gate = jnp.dot(normed, in_weight[0], preferred_element_type=jnp.float32)
    out_gate = jnp.dot(normed, in_weight[1], preferred_element_type=jnp.float32)
    value_proj = jnp.dot(normed, in_weight[2], preferred_element_type=jnp.float32)
    window_value = first_gate * value_proj
    blocks = prefix_values.reshape(N_CTX, PROMPT_DEV, D)

    def accumulate(states, packed):
        block_values, block_id = packed
        distance = (PROMPT + TAIL - (block_id * PROMPT_DEV + jnp.arange(PROMPT_DEV))).astype(jnp.float32)
        return (states + mode_states(block_values, distance, mode_rates), None)
    states, unused = lax.scan(accumulate, jnp.zeros((MODES, D), jnp.float32), (blocks, jnp.arange(N_CTX)))
    prefix_part = expand_states(states, mode_residues, mode_rates, W)
    near_taps = filter_taps(mode_residues, mode_rates, TAIL + W)
    toeplitz = lag_toeplitz(near_taps, TAIL, W)
    live = jnp.arange(TAIL)[None, :] < tail_lengths[:, None]
    tail_live = jnp.where(live[:, :, None], tail_values.astype(jnp.float32), 0.0)
    window_rows = window_value.reshape(BRANCHES, W, D)
    branch_values = jnp.concatenate([tail_live, window_rows], axis=1)
    branch_conv = jnp.einsum('jpc,bpc->bjc', toeplitz, branch_values.astype(jnp.float32))
    combined = out_gate.reshape(BRANCHES, W, D) * (branch_conv + prefix_part[None] + skip_gain * window_rows)
    mixer_in = combined.reshape(ROWS, D).astype(jnp.bfloat16)
    mixed = resid.astype(jnp.float32) + jnp.dot(mixer_in, out_weight, preferred_element_type=jnp.float32)
    normed_mlp = rms_scale(mixed, mlp_gain)
    gate = jnp.dot(normed_mlp, gate_weight, preferred_element_type=jnp.float32)
    up_part = jnp.dot(normed_mlp, up_weight, preferred_element_type=jnp.float32)
    hidden = (jax.nn.silu(gate) * up_part).astype(jnp.bfloat16)
    return (mixed + jnp.dot(hidden, down_weight, preferred_element_type=jnp.float32)).astype(jnp.bfloat16)
```

```python
import functools
import jax
import jax.numpy as jnp
from jax import lax
from jax.experimental import pallas as pl
from jax.experimental.pallas import tpu as pltpu
from jax.sharding import PartitionSpec as P

W = 16
EPS = 1e-05
F32 = jnp.float32
BF16 = jnp.bfloat16
MESH = pl.DeviceIdType.MESH
SEGMENTS = 4


def rms_scale(values, gain):
    values = values.astype(jnp.float32)
    inverse = lax.rsqrt(jnp.mean(values * values, axis=-1, keepdims=True) + 1e-05)
    return (values * inverse * gain).astype(jnp.bfloat16)


def filter_taps(residues, rates, length):
    lags = jnp.arange(length).astype(jnp.float32)
    weights = residues * jnp.sqrt(rates)
    result = jnp.zeros((length, residues.shape[1]), jnp.float32)
    for mode in range(residues.shape[0]):
        result = result + weights[mode][None, :] * jnp.exp(-rates[mode][None, :] * lags[:, None])
    return result


def lag_toeplitz(near_taps, tail_slots, window):
    positions = tail_slots + window
    row_pos = jnp.arange(window)[:, None, None]
    col_pos = jnp.arange(positions)[None, :, None]
    lag_pos = jnp.arange(positions)[None, None, :]
    picked = (lag_pos == tail_slots + row_pos - col_pos) & (col_pos <= tail_slots + row_pos)
    return jnp.einsum("jpn,nc->jpc", picked.astype(jnp.float32), near_taps)


def mode_states(values, distance, rates):
    stacked = []
    for mode in range(rates.shape[0]):
        stacked.append(jnp.sum(jnp.exp(-rates[mode][None, :] * distance[:, None]) * values, axis=0))
    return jnp.stack(stacked)


def expand_states(states, residues, rates, window):
    lags = jnp.arange(window).astype(jnp.float32)
    weights = residues * jnp.sqrt(rates) * states
    result = jnp.zeros((window, states.shape[1]), jnp.float32)
    for mode in range(states.shape[0]):
        result = result + weights[mode][None, :] * jnp.exp(-rates[mode][None, :] * lags[:, None])
    return result


def on_device_plain(
    resid,
    prefix_values,
    tail_values,
    tail_lengths,
    norm_gain,
    in_weight,
    skip_gain,
    mode_residues,
    mode_rates,
    out_weight,
    mlp_gain,
    gate_weight,
    up_weight,
    down_weight,
):
    devices = lax.axis_size("ctx")
    my_index = lax.axis_index("ctx")
    own_width = resid.shape[1]
    row_count = resid.shape[0]
    prompt_rows = prefix_values.shape[0]
    tail_slots = tail_values.shape[1]
    branch_count = tail_values.shape[0]
    first_col = my_index * own_width
    gathered = lax.all_gather(resid, "ctx", axis=1, tiled=True)
    normed = rms_scale(gathered, norm_gain)
    first_gate = jnp.dot(normed, in_weight[0], preferred_element_type=jnp.float32)
    out_gate = jnp.dot(normed, in_weight[1], preferred_element_type=jnp.float32)
    value_proj = jnp.dot(normed, in_weight[2], preferred_element_type=jnp.float32)
    window_value = first_gate * value_proj
    prompt_total = prompt_rows * devices
    distance = (
        prompt_total + tail_slots - (my_index * prompt_rows + jnp.arange(prompt_rows))
    ).astype(jnp.float32)
    states = mode_states(prefix_values, distance, mode_rates)
    residues_own = lax.dynamic_slice_in_dim(mode_residues, first_col, own_width, 1)
    rates_own = lax.dynamic_slice_in_dim(mode_rates, first_col, own_width, 1)
    own_states = lax.psum_scatter(states, "ctx", scatter_dimension=1, tiled=True)
    prefix_part = expand_states(own_states, residues_own, rates_own, W)
    near_taps = filter_taps(residues_own, rates_own, tail_slots + W)
    toeplitz = lag_toeplitz(near_taps, tail_slots, W)
    live = jnp.arange(tail_slots)[None, :] < tail_lengths[:, None]
    tail_live = jnp.where(live[:, :, None], tail_values.astype(jnp.float32), 0.0)
    window_rows = window_value.reshape(branch_count, W, own_width)
    branch_values = jnp.concatenate([tail_live, window_rows], axis=1)
    branch_conv = jnp.einsum("jpc,bpc->bjc", toeplitz, branch_values)
    skip_own = lax.dynamic_slice_in_dim(skip_gain, first_col, own_width)
    combined = out_gate.reshape(branch_count, W, own_width) * (
        branch_conv + prefix_part[None] + skip_own * window_rows
    )
    mixer_in = combined.reshape(row_count, own_width).astype(jnp.bfloat16)
    mixed = resid.astype(jnp.float32) + jnp.dot(
        lax.all_gather(mixer_in, "ctx", axis=1, tiled=True),
        out_weight,
        preferred_element_type=jnp.float32,
    )
    mixed_squares = lax.psum(jnp.sum(mixed * mixed, axis=1), "ctx")
    mixed_inverse = lax.rsqrt(mixed_squares / norm_gain.shape[0] + 1e-05)
    mlp_gain_own = lax.dynamic_slice_in_dim(mlp_gain, first_col, own_width)
    normed_mlp = (mixed * mixed_inverse[:, None] * mlp_gain_own[None, :]).astype(jnp.bfloat16)
    portion = lax.all_gather(normed_mlp, "ctx", axis=1, tiled=True)
    gate = jnp.dot(portion, gate_weight, preferred_element_type=jnp.float32)
    up_part = jnp.dot(portion, up_weight, preferred_element_type=jnp.float32)
    hidden = (jax.nn.silu(gate) * up_part).astype(jnp.bfloat16)
    product = jnp.dot(hidden, down_weight, preferred_element_type=jnp.float32)
    own_cols = lax.dynamic_slice_in_dim(product, first_col, own_width, 1) + mixed
    total = lax.psum_scatter(
        lax.dynamic_update_slice_in_dim(product, own_cols, first_col, 1),
        "ctx",
        scatter_dimension=0,
        tiled=True,
    )
    return total.astype(jnp.bfloat16)


def dot(a, b):
    return jnp.dot(a, b, preferred_element_type=F32)


def line_order(z, nz, t):
    both = jnp.minimum(z, nz - 1 - z)
    near_step = (t + 1) // 2
    near_pos = jnp.where(t % 2 == 1, z + near_step, z - near_step)
    far_pos = jnp.where(2 * z >= nz, z - (t - both), z + (t - both))
    return jnp.where(t <= 2 * both, near_pos, far_pos)


def kernel(
    n,
    resid,
    prefix,
    tail,
    tail_lengths,
    norm_gain,
    in_weight,
    skip_gain,
    residues,
    rates,
    out_weight,
    mlp_gain,
    gate_weight,
    up_weight,
    down_weight,
    out,
    w_a,
    w_b,
    w_o,
    g1,
    g2,
    acc,
    ssq,
    prefix_v,
    prefix_f,
    tail_f,
    taps,
    conv,
    st_send,
    st_recv,
    mixed,
    hidden,
    r1,
    r2,
    ru,
    rd,
    in_sem,
    load_sem,
    down_sem,
    ag_send,
    ag_recv,
    st_ssem,
    st_rsem,
    s1,
    q1,
    s2,
    q2,
    su,
    qu,
    sd,
    qd,
):
    nz = n // 4
    rows, width = resid.shape
    prompt = prefix.shape[0]
    branches, slots = tail.shape[0], tail.shape[1]
    modes = rates.shape[0]
    total_d = n * width
    out_rows = rows // n
    hid = hidden.shape[1]
    ring = w_o.shape[0] // hid
    per_step = branches // n
    me = lax.axis_index("ctx")
    core = me % 2
    x = (me // 2) % 2
    z = me // 4
    sibling = z * 4 + x * 2 + (1 - core)
    across = z * 4 + (1 - x) * 2 + core
    above = me + 4
    below = me - 4
    has_above = z < nz - 1
    has_below = z > 0

    def cols(i):
        return pl.ds(pl.multiple_of(i * width, width), width)

    def remote(src, dst, ssem, rsem, target):
        return pltpu.make_async_remote_copy(
            src_ref=src,
            dst_ref=dst,
            send_sem=ssem,
            recv_sem=rsem,
            device_id={"ctx": target},
            device_id_type=MESH,
        )

    def step_block(m, r):
        t = m - r % 2
        valid = (t >= 0) & (t < nz)
        zt = line_order(z, nz, jnp.clip(t, 0, nz - 1))
        xx = jnp.where(r % 2 == 0, x, 1 - x)
        cc = jnp.where(r < 2, core, 1 - core)
        return valid, zt, zt * 4 + xx * 2 + cc

    def in_load(o):
        return pltpu.make_async_copy(
            in_weight.at[:, pl.ds(pl.multiple_of(o * width, width), width), :],
            w_a.at[:, pl.ds(pl.multiple_of(o * width, width), width), :],
            in_sem.at[o],
        )

    resid_load = pltpu.make_async_copy(resid, g1.at[me], load_sem.at[0])
    prefix_load = pltpu.make_async_copy(prefix, prefix_v, load_sem.at[1])
    out_load = pltpu.make_async_copy(out_weight, w_o, load_sem.at[2])
    mlp_loads = [
        pltpu.make_async_copy(gate_weight.at[:, :width], w_a.at[0], load_sem.at[3]),
        pltpu.make_async_copy(gate_weight.at[:, width:], w_a.at[1], load_sem.at[4]),
        pltpu.make_async_copy(up_weight.at[:, :width], w_a.at[2], load_sem.at[5]),
        pltpu.make_async_copy(up_weight.at[:, width:], w_b, load_sem.at[6]),
    ]

    def down_load(k):
        slot = k % ring
        return pltpu.make_async_copy(
            down_weight.at[:, cols(k)],
            w_o.at[pl.ds(pl.multiple_of(slot * hid, hid), hid), :],
            down_sem.at[slot],
        )

    resid_load.start()
    prefix_load.start()

    @pl.loop(0, nz + 1)
    def _(m):
        @pl.loop(0, 4)
        def _(r):
            valid, _, o = step_block(m, r)

            @pl.when(valid)
            def _():
                in_load(o).start()

    out_load.start()
    mlp_loads[3].start()

    barrier = pltpu.get_barrier_semaphore()

    @pl.loop(1, n)
    def _(d):
        pl.semaphore_signal(
            barrier, inc=1, device_id={"ctx": (me + d) % n}, device_id_type=MESH
        )

    own_rates = rates[:, cols(me)]
    own_weights = residues[:, cols(me)] * jnp.sqrt(own_rates)
    taps[pl.ds(0, W), :] = jnp.zeros((W, width), F32)
    for first in range(0, slots + W, W):
        lags = (first + lax.broadcasted_iota(jnp.int32, (W, width), 0)).astype(F32)
        value = jnp.zeros((W, width), F32)
        for k in range(modes):
            value = value + own_weights[k : k + 1] * jnp.exp(-own_rates[k : k + 1] * lags)
        taps[pl.ds(W + first, W), :] = value

    resid_load.wait()
    pl.semaphore_wait(barrier, n - 1)

    def gather(index, buf, consume):
        def copies(o):
            def to(direction, target):
                return remote(
                    buf.at[o],
                    buf.at[o],
                    ag_send.at[index * 4 + direction, o],
                    ag_recv.at[index, o],
                    target,
                )

            return to(0, above), to(1, below), to(2, across), to(3, sibling)

        @pl.loop(0, nz + 1)
        def _(m):
            @pl.loop(0, 4)
            def _(r):
                valid, zt, o = step_block(m, r)

                @pl.when(valid)
                def _():
                    up, down, over, side = copies(o)

                    @pl.when(o != me)
                    def _():
                        up.wait_recv()

                    @pl.when((r == 0) & (zt <= z) & has_above)
                    def _():
                        up.start()

                    @pl.when((r == 0) & (zt >= z) & has_below)
                    def _():
                        down.start()

                    @pl.when(r == 0)
                    def _():
                        over.start()

                    @pl.when(r < 2)
                    def _():
                        side.start()

                    consume(o)

        @pl.loop(0, nz + 1)
        def _(m):
            @pl.loop(0, 2)
            def _(r):
                valid, zt, o = step_block(m, r)

                @pl.when(valid)
                def _():
                    up, down, over, side = copies(o)

                    @pl.when((r == 0) & (zt <= z) & has_above)
                    def _():
                        up.wait_send()

                    @pl.when((r == 0) & (zt >= z) & has_below)
                    def _():
                        down.wait_send()

                    @pl.when(r == 0)
                    def _():
                        over.wait_send()

                    side.wait_send()

    def state_copy(o, source):
        return remote(
            st_send.at[o], st_recv.at[source], st_ssem.at[o], st_rsem.at[source], o
        )

    acc[...] = jnp.zeros_like(acc)
    ssq[...] = jnp.zeros_like(ssq)
    prefix_load.wait()
    last_distance = (n * prompt + slots - (me * prompt + prompt - 1)).astype(F32)
    seg = prompt // SEGMENTS

    def consume_in(o):
        in_load(o).wait()
        at = pl.ds(pl.multiple_of(o * width, width), width)
        values = g1[o].astype(F32)
        ssq[...] += jnp.sum(values * values, axis=1, keepdims=True)
        scaled = (values * norm_gain[:, cols(o)]).astype(BF16)
        for i in range(3):
            acc[:, i * width : (i + 1) * width] += dot(scaled, w_a[i, at, :])
        rate = rates[:, cols(o)]
        q = jnp.exp(-rate)
        prefix_f[...] = prefix_v[:, cols(o)].astype(F32)

        def horner(s8, parts):
            for u in range(8):
                parts = tuple(
                    part * q + prefix_f[pl.ds(g * seg + s8 * 8 + u, 1), :]
                    for g, part in enumerate(parts)
                )
            return parts

        zero = jnp.zeros((modes, width), F32)
        parts = lax.fori_loop(0, seg // 8, horner, (zero,) * SEGMENTS)
        q_seg = jnp.exp(-rate * float(seg))
        state = parts[0]
        for part in parts[1:]:
            state = state * q_seg + part
        st_send[o] = state * jnp.exp(-rate * last_distance)

        @pl.when(o != me)
        def _():
            state_copy(o, me).start()

        for i in range(per_step):
            b = o * per_step + i
            live = lax.broadcasted_iota(jnp.int32, (slots, width), 0) < tail_lengths[b]
            tail_f[...] = jnp.where(live, tail[b].astype(F32), 0.0)
            y = jnp.zeros((W, width), F32)
            for p in range(slots):
                y = y + taps[pl.ds(W + slots - p, W), :] * tail_f[p : p + 1, :]
            conv[b] = y

    gather(0, g1, consume_in)
    for load in mlp_loads[:3]:
        load.start()

    @pl.loop(1, n)
    def _(d):
        source = (me + d) % n
        state_copy(source, source).wait_recv()
        state_copy(source, source).wait_send()

    st_recv[me] = st_send[me]
    states = st_recv[0]
    for i in range(1, n):
        states = states + st_recv[i]
    states = states * own_weights
    lags = lax.broadcasted_iota(jnp.int32, (W, width), 0).astype(F32)
    part = jnp.zeros((W, width), F32)
    for k in range(modes):
        part = part + states[k : k + 1] * jnp.exp(-own_rates[k : k + 1] * lags)
    taps[pl.ds(slots + W, W), :] = part
    ssq[...] = lax.rsqrt(ssq[...] / float(total_d) + EPS)
    skip = skip_gain[:, cols(me)]

    @pl.loop(0, branches)
    def _(b):
        at = pl.ds(pl.multiple_of(b * W, W), W)
        inverse = ssq[at, :]
        window = (acc[at, 0:width] * inverse) * (acc[at, 2 * width : 3 * width] * inverse)
        tail_f[pl.ds(0, W), :] = window
        y = conv[b] + taps[pl.ds(slots + W, W), :] + skip * window
        for p in range(W):
            y = y + taps[pl.ds(W - p, W), :] * tail_f[p : p + 1, :]
        y = y * (acc[at, width : 2 * width] * inverse)
        mixed[at, :] = y

    g2[me] = mixed[...].astype(BF16).reshape(g2.shape[1:])

    out_load.wait()
    mixed[...] = g1[me].astype(F32)

    def consume_out(o):
        at = pl.ds(pl.multiple_of(o * width, width), width)
        mixed[...] += dot(g2[o].reshape(rows, width), w_o[at, :])

    gather(1, g2, consume_out)
    for k in range(ring):
        down_load(k).start()
    g1[me] = mixed[...].astype(BF16)

    acc[...] = jnp.zeros_like(acc)
    ssq[...] = jnp.zeros_like(ssq)
    for load in mlp_loads:
        load.wait()

    def consume_mlp(o):
        at = pl.ds(pl.multiple_of(o * width, width), width)
        values = g1[o].astype(F32)
        ssq[...] += jnp.sum(values * values, axis=1, keepdims=True)
        scaled = (values * mlp_gain[:, cols(o)]).astype(BF16)
        for i in range(3):
            acc[:, i * width : (i + 1) * width] += dot(scaled, w_a[i, at, :])
        acc[:, 3 * width :] += dot(scaled, w_b[at, :])

    gather(2, g1, consume_mlp)
    ssq[...] = lax.rsqrt(ssq[...] / float(total_d) + EPS)

    @pl.loop(0, rows // 32)
    def _(i):
        at = pl.ds(pl.multiple_of(i * 32, 32), 32)
        inverse = ssq[at, :]
        gate = acc[at, :hid] * inverse
        up = acc[at, hid:] * inverse
        hidden[at, :] = (gate / (1.0 + jnp.exp(-gate)) * up).astype(BF16)

    def core_copy(k):
        return remote(g2.at[k, :, :, 1 - core], r1.at[k], s1.at[k], q1.at[k], sibling)

    def across_copy(k):
        return remote(g2.at[k, :, 1 - x, core], r2.at[k], s2.at[k], q2.at[k], across)

    def up_copy(k, d):
        return remote(
            g2.at[k, d, x, core], ru.at[k, d], su.at[k, d], qu.at[k, d], above
        )

    def down_copy(k, d):
        return remote(
            g2.at[k, d, x, core], rd.at[k, d], sd.at[k, d], qd.at[k, d], below
        )

    def add_into(k, d, arrived):
        g2[k, d, x, core] = (
            g2[k, d, x, core].astype(F32) + arrived.astype(F32)
        ).astype(BF16)

    def stage(k, body):
        @pl.when((k >= 0) & (k < n))
        def _():
            body(k)

    def multiply(k):
        down_load(k).wait()
        slot = k % ring
        at = pl.ds(pl.multiple_of(slot * hid, hid), hid)
        own = jnp.where(k == me, 1.0, 0.0).astype(F32)
        product = dot(hidden[...], w_o[at, :]) + own * mixed[...]
        g2[k] = product.astype(BF16).reshape(g2.shape[1:])
        core_copy(k).start()

        @pl.when(k + ring < n)
        def _():
            down_load(k + ring).start()

    def sum_cores(k):
        core_copy(k).wait_recv()
        for d in range(nz):
            for xx in range(2):
                g2[k, d, xx, core] = (
                    g2[k, d, xx, core].astype(F32) + r1[k, d, xx].astype(F32)
                ).astype(BF16)
        across_copy(k).start()

    def sum_across(k):
        across_copy(k).wait_recv()
        for d in range(nz):
            add_into(k, d, r2[k, d])

    def send_up(k):
        for d in range(1, nz):

            @pl.when((z < d) & has_below)
            def _():
                up_copy(k, d).wait_recv()
                add_into(k, d, ru[k, d])

            @pl.when(z < d)
            def _():
                up_copy(k, d).start()

    def send_down(k):
        for d in range(nz - 1):

            @pl.when((z > d) & has_above)
            def _():
                down_copy(k, d).wait_recv()
                add_into(k, d, rd[k, d])

            @pl.when(z > d)
            def _():
                down_copy(k, d).start()

    def finish(k):
        @pl.when(has_below)
        def _():
            up_copy(k, z).wait_recv()
            add_into(k, z, ru[k, z])

        @pl.when(has_above)
        def _():
            down_copy(k, z).wait_recv()
            add_into(k, z, rd[k, z])

        out[:, cols(k)] = g2[k, z, x, core]

    @pl.loop(0, n + nz + 3)
    def _(i):
        stage(i, multiply)
        stage(i - 1, sum_cores)
        stage(i - 2, sum_across)
        stage(i - 2 - z, send_up)
        stage(i - 2 - (nz - 1 - z), send_down)
        stage(i - 2 - nz, finish)

    @pl.loop(0, n)
    def _(k):
        core_copy(k).wait_send()
        across_copy(k).wait_send()
        for d in range(1, nz):

            @pl.when(z < d)
            def _():
                up_copy(k, d).wait_send()

        for d in range(nz - 1):

            @pl.when(z > d)
            def _():
                down_copy(k, d).wait_send()


def on_device_kernel(*args):
    n = lax.axis_size("ctx")
    (resid, prefix, tail, lengths, norm_gain, in_weight, skip_gain, residues, rates) = args[:9]
    (out_weight, mlp_gain, gate_weight, up_weight, down_weight) = args[9:]
    rows, width = resid.shape
    hid = down_weight.shape[0]
    total = n * width
    modes = rates.shape[0]
    nz = n // 4
    slots = tail.shape[1]
    prompt = prefix.shape[0]
    out_rows = rows // n
    dma = pltpu.SemaphoreType.DMA
    vmem = pl.BlockSpec(memory_space=pltpu.VMEM)
    hbm = pl.BlockSpec(memory_space=pl.ANY)
    smem = pl.BlockSpec(memory_space=pltpu.SMEM)
    flops = 2 * rows * (3 * total * width + total * width + 3 * total * hid)
    return pl.pallas_call(
        functools.partial(kernel, n),
        out_shape=jax.ShapeDtypeStruct((out_rows, total), BF16),
        in_specs=[
            hbm, hbm, vmem, smem, vmem, hbm, vmem, vmem, vmem, hbm, vmem, hbm, hbm, hbm,
        ],
        out_specs=vmem,
        scratch_shapes=[
            pltpu.VMEM((3, total, width), BF16),
            pltpu.VMEM((total, width), BF16),
            pltpu.VMEM((total, width), BF16),
            pltpu.VMEM((n, rows, width), BF16),
            pltpu.VMEM((n, nz, 2, 2, out_rows, width), BF16),
            pltpu.VMEM((rows, 4 * width), F32),
            pltpu.VMEM((rows, 1), F32),
            pltpu.VMEM((prompt, total), BF16),
            pltpu.VMEM((prompt, width), F32),
            pltpu.VMEM((slots, width), F32),
            pltpu.VMEM((slots + 2 * W, width), F32),
            pltpu.VMEM((tail.shape[0], W, width), F32),
            pltpu.VMEM((n, modes, width), F32),
            pltpu.VMEM((n, modes, width), F32),
            pltpu.VMEM((rows, width), F32),
            pltpu.VMEM((rows, hid), BF16),
            pltpu.VMEM((n, nz, 2, out_rows, width), BF16),
            pltpu.VMEM((n, nz, out_rows, width), BF16),
            pltpu.VMEM((n, nz, out_rows, width), BF16),
            pltpu.VMEM((n, nz, out_rows, width), BF16),
            dma((n,)),
            dma((7,)),
            dma((total // hid,)),
            dma((12, n)),
            dma((3, n)),
            dma((n,)),
            dma((n,)),
            dma((n,)),
            dma((n,)),
            dma((n,)),
            dma((n,)),
            dma((n, nz)),
            dma((n, nz)),
            dma((n, nz)),
            dma((n, nz)),
        ],
        compiler_params=pltpu.CompilerParams(
            collective_id=0,
            has_side_effects=True,
            vmem_limit_bytes=63 * 1024 * 1024,
        ),
        cost_estimate=pl.CostEstimate(
            flops=flops, bytes_accessed=flops // rows, transcendentals=0
        ),
    )(
        resid,
        prefix,
        tail,
        lengths,
        norm_gain[None, :],
        in_weight,
        skip_gain[None, :],
        residues,
        rates,
        out_weight,
        mlp_gain[None, :],
        gate_weight,
        up_weight,
        down_weight,
    )


def fits_kernel(args):
    n = lax.axis_size("ctx")
    rows, width = args[0].shape
    hid, total = args[13].shape
    branches, slots = args[2].shape[:2]
    prompt = args[1].shape[0]
    return (
        n % 4 == 0
        and n >= 8
        and width % 128 == 0
        and rows % n == 0
        and (rows // n) % 16 == 0
        and hid == 2 * width
        and (total // hid) <= n
        and branches % n == 0
        and slots % 16 == 0
        and slots >= W
        and prompt % (8 * SEGMENTS) == 0
    )


def on_device(*args):
    if fits_kernel(args):
        return on_device_kernel(*args)
    return on_device_plain(*args)


def solution(mesh):
    return jax.shard_map(
        on_device,
        mesh=mesh,
        in_specs=(
            P("rep", "ctx"),
            P(("rep", "ctx"), None),
            P("rep", None, "ctx"),
            P("rep"),
            P(),
            P(None, None, "ctx"),
            P(),
            P(),
            P(),
            P(None, "ctx"),
            P(),
            P(None, "ctx"),
            P(None, "ctx"),
            P("ctx", None),
        ),
        out_specs=P(("rep", "ctx"), None),
        check_vma=False,
    )
```

```python
import functools
import jax
import jax.numpy as jnp
from jax import lax
from jax.experimental import pallas as pl
from jax.experimental.pallas import tpu as pltpu
from jax.sharding import PartitionSpec as P

W = 16
EPS = 1e-05
F32 = jnp.float32
BF16 = jnp.bfloat16
MESH = pl.DeviceIdType.MESH
SEGMENTS = 4


def rms_scale(values, gain):
    values = values.astype(jnp.float32)
    inverse = lax.rsqrt(jnp.mean(values * values, axis=-1, keepdims=True) + 1e-05)
    return (values * inverse * gain).astype(jnp.bfloat16)


def filter_taps(residues, rates, length):
    lags = jnp.arange(length).astype(jnp.float32)
    weights = residues * jnp.sqrt(rates)
    result = jnp.zeros((length, residues.shape[1]), jnp.float32)
    for mode in range(residues.shape[0]):
        result = result + weights[mode][None, :] * jnp.exp(-rates[mode][None, :] * lags[:, None])
    return result


def lag_toeplitz(near_taps, tail_slots, window):
    positions = tail_slots + window
    row_pos = jnp.arange(window)[:, None, None]
    col_pos = jnp.arange(positions)[None, :, None]
    lag_pos = jnp.arange(positions)[None, None, :]
    picked = (lag_pos == tail_slots + row_pos - col_pos) & (col_pos <= tail_slots + row_pos)
    return jnp.einsum("jpn,nc->jpc", picked.astype(jnp.float32), near_taps)


def mode_states(values, distance, rates):
    stacked = []
    for mode in range(rates.shape[0]):
        stacked.append(jnp.sum(jnp.exp(-rates[mode][None, :] * distance[:, None]) * values, axis=0))
    return jnp.stack(stacked)


def expand_states(states, residues, rates, window):
    lags = jnp.arange(window).astype(jnp.float32)
    weights = residues * jnp.sqrt(rates) * states
    result = jnp.zeros((window, states.shape[1]), jnp.float32)
    for mode in range(states.shape[0]):
        result = result + weights[mode][None, :] * jnp.exp(-rates[mode][None, :] * lags[:, None])
    return result


def on_device_plain(
    resid,
    prefix_values,
    tail_values,
    tail_lengths,
    norm_gain,
    in_weight,
    skip_gain,
    mode_residues,
    mode_rates,
    out_weight,
    mlp_gain,
    gate_weight,
    up_weight,
    down_weight,
):
    devices = lax.axis_size("ctx")
    my_index = lax.axis_index("ctx")
    own_width = resid.shape[1]
    row_count = resid.shape[0]
    prompt_rows = prefix_values.shape[0]
    tail_slots = tail_values.shape[1]
    branch_count = tail_values.shape[0]
    first_col = my_index * own_width
    gathered = lax.all_gather(resid, "ctx", axis=1, tiled=True)
    normed = rms_scale(gathered, norm_gain)
    first_gate = jnp.dot(normed, in_weight[0], preferred_element_type=jnp.float32)
    out_gate = jnp.dot(normed, in_weight[1], preferred_element_type=jnp.float32)
    value_proj = jnp.dot(normed, in_weight[2], preferred_element_type=jnp.float32)
    window_value = first_gate * value_proj
    prompt_total = prompt_rows * devices
    distance = (
        prompt_total + tail_slots - (my_index * prompt_rows + jnp.arange(prompt_rows))
    ).astype(jnp.float32)
    states = mode_states(prefix_values, distance, mode_rates)
    residues_own = lax.dynamic_slice_in_dim(mode_residues, first_col, own_width, 1)
    rates_own = lax.dynamic_slice_in_dim(mode_rates, first_col, own_width, 1)
    own_states = lax.psum_scatter(states, "ctx", scatter_dimension=1, tiled=True)
    prefix_part = expand_states(own_states, residues_own, rates_own, W)
    near_taps = filter_taps(residues_own, rates_own, tail_slots + W)
    toeplitz = lag_toeplitz(near_taps, tail_slots, W)
    live = jnp.arange(tail_slots)[None, :] < tail_lengths[:, None]
    tail_live = jnp.where(live[:, :, None], tail_values.astype(jnp.float32), 0.0)
    window_rows = window_value.reshape(branch_count, W, own_width)
    branch_values = jnp.concatenate([tail_live, window_rows], axis=1)
    branch_conv = jnp.einsum("jpc,bpc->bjc", toeplitz, branch_values)
    skip_own = lax.dynamic_slice_in_dim(skip_gain, first_col, own_width)
    combined = out_gate.reshape(branch_count, W, own_width) * (
        branch_conv + prefix_part[None] + skip_own * window_rows
    )
    mixer_in = combined.reshape(row_count, own_width).astype(jnp.bfloat16)
    mixed = resid.astype(jnp.float32) + jnp.dot(
        lax.all_gather(mixer_in, "ctx", axis=1, tiled=True),
        out_weight,
        preferred_element_type=jnp.float32,
    )
    mixed_squares = lax.psum(jnp.sum(mixed * mixed, axis=1), "ctx")
    mixed_inverse = lax.rsqrt(mixed_squares / norm_gain.shape[0] + 1e-05)
    mlp_gain_own = lax.dynamic_slice_in_dim(mlp_gain, first_col, own_width)
    normed_mlp = (mixed * mixed_inverse[:, None] * mlp_gain_own[None, :]).astype(jnp.bfloat16)
    portion = lax.all_gather(normed_mlp, "ctx", axis=1, tiled=True)
    gate = jnp.dot(portion, gate_weight, preferred_element_type=jnp.float32)
    up_part = jnp.dot(portion, up_weight, preferred_element_type=jnp.float32)
    hidden = (jax.nn.silu(gate) * up_part).astype(jnp.bfloat16)
    product = jnp.dot(hidden, down_weight, preferred_element_type=jnp.float32)
    own_cols = lax.dynamic_slice_in_dim(product, first_col, own_width, 1) + mixed
    total = lax.psum_scatter(
        lax.dynamic_update_slice_in_dim(product, own_cols, first_col, 1),
        "ctx",
        scatter_dimension=0,
        tiled=True,
    )
    return total.astype(jnp.bfloat16)


def dot(a, b):
    return jnp.dot(a, b, preferred_element_type=F32)


def line_order(z, nz, t):
    both = jnp.minimum(z, nz - 1 - z)
    near_step = (t + 1) // 2
    near_pos = jnp.where(t % 2 == 1, z - near_step, z + near_step)
    far_pos = jnp.where(2 * z >= nz, z - (t - both), z + (t - both))
    return jnp.where(t <= 2 * both, near_pos, far_pos)


def kernel(
    n,
    resid,
    prefix,
    tail,
    tail_lengths,
    norm_gain,
    in_weight,
    skip_gain,
    residues,
    rates,
    out_weight,
    mlp_gain,
    gate_weight,
    up_weight,
    down_weight,
    out,
    w_a,
    w_b,
    w_o,
    g1,
    g2,
    acc,
    ssq,
    prefix_v,
    prefix_f,
    tail_f,
    taps,
    conv,
    st_send,
    st_recv,
    mixed,
    hidden,
    r1,
    r2,
    ru,
    in_sem,
    load_sem,
    down_sem,
    ag_send,
    ag_recv,
    st_ssem,
    st_rsem,
    s1,
    q1,
    s2,
    q2,
    su,
    qu,
):
    nz = n // 4
    rows, width = resid.shape
    prompt = prefix.shape[0]
    branches, slots = tail.shape[0], tail.shape[1]
    modes = rates.shape[0]
    total_d = n * width
    out_rows = rows // n
    hid = hidden.shape[1]
    ring = w_o.shape[0] // hid
    per_step = branches // n
    me = lax.axis_index("ctx")
    core = me % 2
    x = (me // 2) % 2
    z = me // 4
    sibling = z * 4 + x * 2 + (1 - core)
    across = z * 4 + (1 - x) * 2 + core
    above = me + 4
    below = me - 4
    has_above = z < nz - 1
    has_below = z > 0

    def cols(i):
        return pl.ds(pl.multiple_of(i * width, width), width)

    def remote(src, dst, ssem, rsem, target):
        return pltpu.make_async_remote_copy(
            src_ref=src,
            dst_ref=dst,
            send_sem=ssem,
            recv_sem=rsem,
            device_id={"ctx": target},
            device_id_type=MESH,
        )

    def step_block(m, r):
        kind = r % 3
        t = jnp.maximum(m - 1, 0)
        zt = jnp.where(
            kind == 0, z - m, jnp.where(kind == 1, z + m, line_order(z, nz, t))
        )
        valid = jnp.where(kind == 1, m > 0, (kind == 0) | (m > 0))
        valid = valid & (zt >= 0) & (zt < nz)
        zt = jnp.clip(zt, 0, nz - 1)
        xx = jnp.where(kind < 2, x, 1 - x)
        cc = jnp.where(r < 3, core, 1 - core)
        return valid, zt, zt * 4 + xx * 2 + cc

    def in_load(o):
        return pltpu.make_async_copy(
            in_weight.at[:, pl.ds(pl.multiple_of(o * width, width), width), :],
            w_a.at[:, pl.ds(pl.multiple_of(o * width, width), width), :],
            in_sem.at[o],
        )

    resid_load = pltpu.make_async_copy(resid, g1.at[me], load_sem.at[0])
    prefix_load = pltpu.make_async_copy(prefix, prefix_v, load_sem.at[1])
    out_load = pltpu.make_async_copy(out_weight, w_o, load_sem.at[2])
    mlp_loads = [
        pltpu.make_async_copy(gate_weight.at[:, :width], w_a.at[0], load_sem.at[3]),
        pltpu.make_async_copy(gate_weight.at[:, width:], w_a.at[1], load_sem.at[4]),
        pltpu.make_async_copy(up_weight.at[:, :width], w_a.at[2], load_sem.at[5]),
        pltpu.make_async_copy(up_weight.at[:, width:], w_b, load_sem.at[6]),
    ]

    def down_load(k):
        slot = k % ring
        return pltpu.make_async_copy(
            down_weight.at[:, cols(k)],
            w_o.at[pl.ds(pl.multiple_of(slot * hid, hid), hid), :],
            down_sem.at[slot],
        )

    resid_load.start()
    prefix_load.start()

    def start_loads(m):
        @pl.loop(0, 6)
        def _(r):
            valid, _, o = step_block(m, r)

            @pl.when(valid)
            def _():
                in_load(o).start()

    def load_ahead(m):
        @pl.when(m < nz)
        def _():
            start_loads(m + 1)

        @pl.when(m == nz - 1)
        def _():
            out_load.start()
            mlp_loads[3].start()

    barrier = pltpu.get_barrier_semaphore()

    @pl.loop(1, n)
    def _(d):
        pl.semaphore_signal(
            barrier, inc=1, device_id={"ctx": (me + d) % n}, device_id_type=MESH
        )

    own_rates = rates[:, cols(me)]
    own_weights = residues[:, cols(me)] * jnp.sqrt(own_rates)
    taps[pl.ds(0, W), :] = jnp.zeros((W, width), F32)
    for first in range(0, slots + W, W):
        lags = (first + lax.broadcasted_iota(jnp.int32, (W, width), 0)).astype(F32)
        value = jnp.zeros((W, width), F32)
        for k in range(modes):
            value = value + own_weights[k : k + 1] * jnp.exp(-own_rates[k : k + 1] * lags)
        taps[pl.ds(W + first, W), :] = value

    resid_load.wait()
    pl.semaphore_wait(barrier, n - 1)
    start_loads(0)

    def gather(index, buf, consume, ahead=None):
        def copies(o):
            def to(direction, target):
                return remote(
                    buf.at[o],
                    buf.at[o],
                    ag_send.at[index * 4 + direction, o],
                    ag_recv.at[index, o],
                    target,
                )

            return to(0, above), to(1, below), to(2, across), to(3, sibling)

        @pl.loop(0, nz + 1)
        def _(m):
            @pl.loop(0, 6)
            def _(r):
                valid, zt, o = step_block(m, r)
                if ahead is not None:
                    pl.when(r == 3)(lambda: ahead(m))

                @pl.when(valid)
                def _():
                    up, down, over, side = copies(o)

                    @pl.when(o != me)
                    def _():
                        up.wait_recv()

                    @pl.when((r < 2) & (zt <= z) & has_above)
                    def _():
                        up.start()

                    @pl.when((r < 2) & (zt >= z) & has_below)
                    def _():
                        down.start()

                    @pl.when(r < 2)
                    def _():
                        over.start()

                    @pl.when(r < 3)
                    def _():
                        side.start()

                    consume(o)

        @pl.loop(0, nz + 1)
        def _(m):
            @pl.loop(0, 3)
            def _(r):
                valid, zt, o = step_block(m, r)

                @pl.when(valid)
                def _():
                    up, down, over, side = copies(o)

                    @pl.when((r < 2) & (zt <= z) & has_above)
                    def _():
                        up.wait_send()

                    @pl.when((r < 2) & (zt >= z) & has_below)
                    def _():
                        down.wait_send()

                    @pl.when(r < 2)
                    def _():
                        over.wait_send()

                    side.wait_send()

    def state_copy(o, source):
        return remote(
            st_send.at[o], st_recv.at[source], st_ssem.at[o], st_rsem.at[source], o
        )

    acc[...] = jnp.zeros_like(acc)
    ssq[...] = jnp.zeros_like(ssq)
    prefix_load.wait()
    last_distance = (n * prompt + slots - (me * prompt + prompt - 1)).astype(F32)
    seg = prompt // SEGMENTS

    def consume_in(o):
        in_load(o).wait()
        at = pl.ds(pl.multiple_of(o * width, width), width)
        values = g1[o].astype(F32)
        ssq[...] += jnp.sum(values * values, axis=1, keepdims=True)
        scaled = (values * norm_gain[:, cols(o)]).astype(BF16)
        for i in range(3):
            acc[:, i * width : (i + 1) * width] += dot(scaled, w_a[i, at, :])
        rate = rates[:, cols(o)]
        q = jnp.exp(-rate)
        prefix_f[...] = prefix_v[:, cols(o)].astype(F32)

        def horner(s8, parts):
            for u in range(8):
                parts = tuple(
                    part * q + prefix_f[pl.ds(g * seg + s8 * 8 + u, 1), :]
                    for g, part in enumerate(parts)
                )
            return parts

        zero = jnp.zeros((modes, width), F32)
        parts = lax.fori_loop(0, seg // 8, horner, (zero,) * SEGMENTS)
        q_seg = jnp.exp(-rate * float(seg))
        state = parts[0]
        for part in parts[1:]:
            state = state * q_seg + part
        st_send[o] = state * jnp.exp(-rate * last_distance)

        @pl.when(o != me)
        def _():
            state_copy(o, me).start()

        for i in range(per_step):
            b = o * per_step + i
            live = lax.broadcasted_iota(jnp.int32, (slots, width), 0) < tail_lengths[b]
            tail_f[...] = jnp.where(live, tail[b].astype(F32), 0.0)
            y = jnp.zeros((W, width), F32)
            for p in range(slots):
                y = y + taps[pl.ds(W + slots - p, W), :] * tail_f[p : p + 1, :]
            conv[b] = y

    gather(0, g1, consume_in, load_ahead)
    for load in mlp_loads[:3]:
        load.start()

    @pl.loop(1, n)
    def _(d):
        source = (me + d) % n
        state_copy(source, source).wait_recv()
        state_copy(source, source).wait_send()

    st_recv[me] = st_send[me]
    states = st_recv[0]
    for i in range(1, n):
        states = states + st_recv[i]
    states = states * own_weights
    lags = lax.broadcasted_iota(jnp.int32, (W, width), 0).astype(F32)
    part = jnp.zeros((W, width), F32)
    for k in range(modes):
        part = part + states[k : k + 1] * jnp.exp(-own_rates[k : k + 1] * lags)
    taps[pl.ds(slots + W, W), :] = part
    ssq[...] = lax.rsqrt(ssq[...] / float(total_d) + EPS)
    skip = skip_gain[:, cols(me)]

    @pl.loop(0, branches)
    def _(b):
        at = pl.ds(pl.multiple_of(b * W, W), W)
        inverse = ssq[at, :]
        window = (acc[at, 0:width] * inverse) * (acc[at, 2 * width : 3 * width] * inverse)
        tail_f[pl.ds(0, W), :] = window
        y = conv[b] + taps[pl.ds(slots + W, W), :] + skip * window
        for p in range(W):
            y = y + taps[pl.ds(W - p, W), :] * tail_f[p : p + 1, :]
        y = y * (acc[at, width : 2 * width] * inverse)
        mixed[at, :] = y

    g2[me] = mixed[...].astype(BF16).reshape(g2.shape[1:])

    out_load.wait()
    mixed[...] = g1[me].astype(F32)

    def consume_out(o):
        at = pl.ds(pl.multiple_of(o * width, width), width)
        mixed[...] += dot(g2[o].reshape(rows, width), w_o[at, :])

    gather(1, g2, consume_out)
    for k in range(ring):
        down_load(k).start()
    g1[me] = mixed[...].astype(BF16)

    acc[...] = jnp.zeros_like(acc)
    ssq[...] = jnp.zeros_like(ssq)
    for load in mlp_loads:
        load.wait()

    def consume_mlp(o):
        at = pl.ds(pl.multiple_of(o * width, width), width)
        values = g1[o].astype(F32)
        ssq[...] += jnp.sum(values * values, axis=1, keepdims=True)
        scaled = (values * mlp_gain[:, cols(o)]).astype(BF16)
        for i in range(3):
            acc[:, i * width : (i + 1) * width] += dot(scaled, w_a[i, at, :])
        acc[:, 3 * width :] += dot(scaled, w_b[at, :])

    gather(2, g1, consume_mlp)
    ssq[...] = lax.rsqrt(ssq[...] / float(total_d) + EPS)

    @pl.loop(0, rows // 32)
    def _(i):
        at = pl.ds(pl.multiple_of(i * 32, 32), 32)
        inverse = ssq[at, :]
        gate = acc[at, :hid] * inverse
        up = acc[at, hid:] * inverse
        hidden[at, :] = (gate / (1.0 + jnp.exp(-gate)) * up).astype(BF16)

    def core_copy(k):
        return remote(g2.at[k, :, :, 1 - core], r1.at[k], s1.at[k], q1.at[k], sibling)

    def across_copy(k):
        return remote(g2.at[k, :, 1 - x, core], r2.at[k], s2.at[k], q2.at[k], across)

    def line_copy(k, d, source):
        return remote(
            g2.at[k, d, x, core],
            ru.at[k, source],
            su.at[k, d],
            qu.at[k, source],
            d * 4 + x * 2 + core,
        )

    def add_into(k, d, arrived):
        g2[k, d, x, core] = (
            g2[k, d, x, core].astype(F32) + arrived.astype(F32)
        ).astype(BF16)

    def stage(k, body):
        @pl.when((k >= 0) & (k < n))
        def _():
            body(k)

    def multiply(k):
        down_load(k).wait()
        slot = k % ring
        at = pl.ds(pl.multiple_of(slot * hid, hid), hid)
        own = jnp.where(k == me, 1.0, 0.0).astype(F32)
        product = dot(hidden[...], w_o[at, :]) + own * mixed[...]
        g2[k] = product.astype(BF16).reshape(g2.shape[1:])
        core_copy(k).start()

        @pl.when(k + ring < n)
        def _():
            down_load(k + ring).start()

    def sum_cores(k):
        core_copy(k).wait_recv()
        for d in range(nz):
            for xx in range(2):
                g2[k, d, xx, core] = (
                    g2[k, d, xx, core].astype(F32) + r1[k, d, xx].astype(F32)
                ).astype(BF16)
        across_copy(k).start()

    def sum_across(k):
        across_copy(k).wait_recv()
        for d in range(nz):
            add_into(k, d, r2[k, d])
        for d in range(nz):

            @pl.when(z != d)
            def _():
                line_copy(k, d, z).start()

    def finish(k):
        ru[k, z] = g2[k, z, x, core]
        for d in range(nz):

            @pl.when(z != d)
            def _():
                line_copy(k, d, d).wait_recv()

        value = ru[k, 0].astype(F32)
        for d in range(1, nz):
            value = value + ru[k, d].astype(F32)
        out[:, cols(k)] = value.astype(BF16)

    @pl.loop(0, n + 6)
    def _(i):
        stage(i, multiply)
        stage(i - 3, sum_across)
        stage(i - 1, sum_cores)
        stage(i - 6, finish)

    @pl.loop(0, n)
    def _(k):
        core_copy(k).wait_send()
        across_copy(k).wait_send()
        for d in range(nz):

            @pl.when(z != d)
            def _():
                line_copy(k, d, z).wait_send()


def on_device_kernel(*args):
    n = lax.axis_size("ctx")
    (resid, prefix, tail, lengths, norm_gain, in_weight, skip_gain, residues, rates) = args[:9]
    (out_weight, mlp_gain, gate_weight, up_weight, down_weight) = args[9:]
    rows, width = resid.shape
    hid = down_weight.shape[0]
    total = n * width
    modes = rates.shape[0]
    nz = n // 4
    slots = tail.shape[1]
    prompt = prefix.shape[0]
    out_rows = rows // n
    dma = pltpu.SemaphoreType.DMA
    vmem = pl.BlockSpec(memory_space=pltpu.VMEM)
    hbm = pl.BlockSpec(memory_space=pl.ANY)
    smem = pl.BlockSpec(memory_space=pltpu.SMEM)
    flops = 2 * rows * (3 * total * width + total * width + 3 * total * hid)
    return pl.pallas_call(
        functools.partial(kernel, n),
        out_shape=jax.ShapeDtypeStruct((out_rows, total), BF16),
        in_specs=[
            hbm, hbm, vmem, smem, vmem, hbm, vmem, vmem, vmem, hbm, vmem, hbm, hbm, hbm,
        ],
        out_specs=vmem,
        scratch_shapes=[
            pltpu.VMEM((3, total, width), BF16),
            pltpu.VMEM((total, width), BF16),
            pltpu.VMEM((total, width), BF16),
            pltpu.VMEM((n, rows, width), BF16),
            pltpu.VMEM((n, nz, 2, 2, out_rows, width), BF16),
            pltpu.VMEM((rows, 4 * width), F32),
            pltpu.VMEM((rows, 1), F32),
            pltpu.VMEM((prompt, total), BF16),
            pltpu.VMEM((prompt, width), F32),
            pltpu.VMEM((slots, width), F32),
            pltpu.VMEM((slots + 2 * W, width), F32),
            pltpu.VMEM((tail.shape[0], W, width), F32),
            pltpu.VMEM((n, modes, width), F32),
            pltpu.VMEM((n, modes, width), F32),
            pltpu.VMEM((rows, width), F32),
            pltpu.VMEM((rows, hid), BF16),
            pltpu.VMEM((n, nz, 2, out_rows, width), BF16),
            pltpu.VMEM((n, nz, out_rows, width), BF16),
            pltpu.VMEM((n, nz, out_rows, width), BF16),
            dma((n,)),
            dma((7,)),
            dma((total // hid,)),
            dma((12, n)),
            dma((3, n)),
            dma((n,)),
            dma((n,)),
            dma((n,)),
            dma((n,)),
            dma((n,)),
            dma((n,)),
            dma((n, nz)),
            dma((n, nz)),
        ],
        compiler_params=pltpu.CompilerParams(
            collective_id=0,
            has_side_effects=True,
            vmem_limit_bytes=63 * 1024 * 1024,
        ),
        cost_estimate=pl.CostEstimate(
            flops=flops, bytes_accessed=flops // rows, transcendentals=0
        ),
    )(
        resid,
        prefix,
        tail,
        lengths,
        norm_gain[None, :],
        in_weight,
        skip_gain[None, :],
        residues,
        rates,
        out_weight,
        mlp_gain[None, :],
        gate_weight,
        up_weight,
        down_weight,
    )


def fits_kernel(args):
    n = lax.axis_size("ctx")
    rows, width = args[0].shape
    hid, total = args[13].shape
    branches, slots = args[2].shape[:2]
    prompt = args[1].shape[0]
    return (
        n % 4 == 0
        and n >= 8
        and width % 128 == 0
        and rows % n == 0
        and (rows // n) % 16 == 0
        and hid == 2 * width
        and (total // hid) <= n
        and branches % n == 0
        and slots % 16 == 0
        and slots >= W
        and prompt % (8 * SEGMENTS) == 0
    )


def on_device(*args):
    if fits_kernel(args):
        return on_device_kernel(*args)
    return on_device_plain(*args)


def solution(mesh):
    return jax.shard_map(
        on_device,
        mesh=mesh,
        in_specs=(
            P("rep", "ctx"),
            P(("rep", "ctx"), None),
            P("rep", None, "ctx"),
            P("rep"),
            P(),
            P(None, None, "ctx"),
            P(),
            P(),
            P(),
            P(None, "ctx"),
            P(),
            P(None, "ctx"),
            P(None, "ctx"),
            P("ctx", None),
        ),
        out_specs=P(("rep", "ctx"), None),
        check_vma=False,
    )
```
